32 devices in a mesh: group: 2 (over x), weight: 16 (over z, y, core).
Axes of the slice: x: 2, y: 2, z: 4, core: 2. Of those that a mesh axis runs over, the one named last changes fastest.
Arguments:
- hidden_in: bfloat16 [1024, 8192], P('group', 'weight'), parts along dimension 0, may hold values from -20 to 20
- norm_gain: bfloat16 [8192], P('weight'), may hold values from 0.5 to 4.5
- w_query: bfloat16 [8192, 8192], P(None, 'weight'), may hold values from -4 to 4
- w_key: bfloat16 [8192, 1024], P(None, 'weight'), may hold values from -4 to 4
- w_value: bfloat16 [8192, 1024], P(None, 'weight'), may hold values from -0.0625 to 0.0625
- w_out: bfloat16 [8192, 8192], P(None, 'weight'), may hold values from -0.0625 to 0.0625
- segment_ids: int32 [1024], P('group'), parts along dimension 0, may hold values from 0 to 31, never falling along the last dimension, each value on 1 to 32 neighbouring positions
Outputs:
- mixed: bfloat16 [1024, 8192], P('group', 'weight'), parts along dimension 0
The draws below stay inside these ranges and needn't reach their ends.
There are 2 independent parts, one for each index of `group`. The reference program is written for one: setup_inputs(seed, part) draws one part's arguments, and reference() takes and returns one part's arrays. A program takes and returns all parts, laid end to end along the dimension named above; an argument that names none is the same for every part. Nothing has to cross between parts.
All inputs are finite; a program needn't handle non-finite values.
Results may differ from the reference program's by a relative error of at most 0.0065.
Values may be sent and summed in bfloat16 or wider, within the bound.
A program may use at most 128 MiB of HBM per device.

```python
import math
import jax
import jax.numpy as jnp
import numpy as np
from jax import lax

D = 8192
QH = 64
KVH = 8
HD = 128
TOKENS = 512
SEGS = 32


def common_base(key):
    sample = jax.random.normal(key, (D, KVH * HD), jnp.float32)
    return jnp.clip(sample, -6.0, 6.0)


def draw_hidden_in(key, part):
    key = jax.random.fold_in(key, 11)
    first_key, second_key = jax.random.split(key, 2)
    sample = jnp.clip(jax.random.normal(first_key, (TOKENS, D), jnp.float32), -6.0, 6.0)
    scales = jnp.exp(jax.random.uniform(second_key, (TOKENS, 1), jnp.float32, jnp.log(0.3), jnp.log(3.0)))
    return (sample * scales).astype(jnp.bfloat16)


def draw_norm_gain(key, part):
    key = jax.random.fold_in(key, 23)
    sample = jax.random.uniform(key, (D,), jnp.float32, 0.5, 1.6)
    return sample.astype(jnp.bfloat16)


def draw_w_key(key, part):
    base = common_base(key)
    return (base / jnp.sqrt(jnp.float32(D))).astype(jnp.bfloat16)


def draw_w_query(key, part):
    key = jax.random.fold_in(key, 41)
    own_key = jax.random.fold_in(key, 0)
    own = jnp.clip(jax.random.normal(own_key, (D, QH * HD), jnp.float32), -6.0, 6.0)
    sample = own
    return (sample / jnp.sqrt(jnp.float32(D))).astype(jnp.bfloat16)


def block_levels(rng, dims, cuts, least, top_value):
    level = 1.0
    for axis_at, parts in cuts:
        steps = jax.random.uniform(jax.random.fold_in(jax.random.fold_in(rng, 6), axis_at), (parts,), jnp.float32, least / len(cuts), top_value / len(cuts))
        level = level * jnp.repeat(jnp.exp(steps), dims[axis_at] // parts).reshape((-1,) + (1,) * (len(dims) - 1 - axis_at))
    return level


def profile(number_of, total, most, lean):
    loads = [(1 << 20) // math.isqrt(rank ** lean) + 1 for rank in range(2, number_of + 1)]
    rest, given = total - most - (number_of - 1), [1] * (number_of - 1)
    while rest > 0:
        free = [i for i in range(number_of - 1) if given[i] < most]
        mass, budget = sum([loads[i] for i in free]), rest
        for i in free:
            more = min(most - given[i], max(1, budget * loads[i] // mass), rest)
            given[i] = given[i] + more
            rest = rest - more
    return np.array([most] + given)


def uneven_parts(rng, number_of, total, reach, slope):
    if number_of == 2:
        one = jax.random.randint(rng, (), max(1, total - reach), min(reach, total - 1) + 1)
        return jnp.stack([one, total - one])
    sizes = jnp.asarray(profile(number_of, total, reach, slope), jnp.int32)
    pairs = (number_of - 1) // 2
    donor, sink = sizes[1:1 + 2 * pairs:2], sizes[2:2 + 2 * pairs:2]
    room = jnp.minimum(donor - 1, reach - sink)
    passed = jax.random.randint(jax.random.fold_in(rng, 1), (pairs,), 0, 1 << 20) % (room + 1)
    sizes = sizes.at[1:1 + 2 * pairs:2].set(donor - passed).at[2:2 + 2 * pairs:2].set(sink + passed)
    return sizes[jax.random.permutation(jax.random.fold_in(rng, 2), number_of)]


def normal_values(key, shape, scale, limit, shards=(), kind=jnp.bfloat16):
    array = jax.random.normal(key, shape, jnp.float32) * scale
    if len(shards) > 0:
        array = block_levels(key, shape, shards, -0.22, 0.18) * array
    return jnp.clip(array, min=-limit, max=limit).astype(kind)


def setup_inputs(seed: int = 0, part: int = 0) -> dict:
    splits = jax.random.split(jax.random.key(seed), 8)
    own_keys = jax.random.split(jax.random.fold_in(splits[7], part), 8)
    return {
        "hidden_in": draw_hidden_in(jax.random.fold_in(jax.random.fold_in(splits[7], part), 71), part),
        "norm_gain": draw_norm_gain(jax.random.fold_in(splits[7], 71), part),
        "w_query": draw_w_query(jax.random.fold_in(splits[7], 71), part),
        "w_key": draw_w_key(jax.random.fold_in(splits[7], 71), part),
        "w_value": normal_values(splits[4], (D, KVH * HD), D ** -0.5, 0.0625, ((1, 16),)),
        "w_out": normal_values(splits[5], (QH * HD, D), (QH * HD) ** -0.5, 0.0625, ((1, 16),)),
        "segment_ids": jnp.searchsorted(jnp.cumsum(uneven_parts(own_keys[6], SEGS, TOKENS, 32, 1)), jnp.arange(TOKENS), side="right").astype(jnp.int32),
    }


def rotate(values, position):
    half = values.shape[-1] // 2
    steps = jnp.arange(half, dtype=jnp.float32)
    freq = jnp.exp(-(2.0 * steps / (2 * half)) * jnp.log(jnp.float32(500000.0)))
    angle = position[:, None] * freq[None, :]
    cosine = jnp.cos(angle)[:, None, :]
    sine = jnp.sin(angle)[:, None, :]
    first = values[..., :half]
    second = values[..., half:]
    return jnp.concatenate([first * cosine - second * sine, second * cosine + first * sine], axis=-1)

def positions_of(segment_ids):
    count = segment_ids.shape[0]
    index = jnp.arange(count, dtype=jnp.int32)
    same = segment_ids[:, None] == segment_ids[None, :]
    start = lax.optimization_barrier(jnp.min(jnp.where(same, index[None, :], count), axis=1))
    return ((index - start).astype(jnp.float32), same)

def reference(hidden_in, norm_gain, w_query, w_key, w_value, w_out, segment_ids):
    as_float = hidden_in.astype(jnp.float32)
    mean_sq = lax.optimization_barrier(jnp.mean(as_float * as_float, axis=1, keepdims=True))
    normed = (as_float * lax.rsqrt(mean_sq + 1e-05) * norm_gain.astype(jnp.float32)[None, :]).astype(jnp.bfloat16)
    query_raw = jnp.dot(normed, w_query, preferred_element_type=jnp.float32)
    key_raw = jnp.dot(normed, w_key, preferred_element_type=jnp.float32).astype(jnp.bfloat16)
    value_raw = jnp.dot(normed, w_value, preferred_element_type=jnp.float32).astype(jnp.bfloat16)
    count = hidden_in.shape[0]
    position, same = positions_of(segment_ids)
    index = jnp.arange(count, dtype=jnp.int32)
    keep = same & (index[None, :] <= index[:, None])
    query = rotate(query_raw.reshape(count, QH, HD), position).astype(jnp.bfloat16)
    key_rot = rotate(key_raw.astype(jnp.float32).reshape(count, KVH, HD), position).astype(jnp.bfloat16)
    key_all = jnp.repeat(key_rot, QH // KVH, axis=1)
    value_all = jnp.repeat(value_raw.reshape(count, KVH, HD), QH // KVH, axis=1)
    scores = jnp.einsum('thd,shd->hts', query.astype(jnp.float32), key_all.astype(jnp.float32)) / jnp.sqrt(jnp.float32(HD))
    scores = jnp.where(keep[None, :, :], scores, -jnp.inf)
    top = lax.optimization_barrier(jnp.max(scores, axis=2, keepdims=True))
    probs = jnp.exp(scores - top)
    total = lax.optimization_barrier(jnp.sum(probs, axis=2))
    weights = probs.astype(jnp.bfloat16)
    summed = jnp.einsum('hts,shd->thd', weights.astype(jnp.float32), value_all.astype(jnp.float32))
    heads = (summed / jnp.transpose(total)[:, :, None]).astype(jnp.bfloat16).reshape(count, QH * HD)
    project = jnp.dot(heads, w_out, preferred_element_type=jnp.float32)
    return (as_float + project).astype(jnp.bfloat16)
```

```python
import functools

import jax
import jax.numpy as jnp
from jax import lax
from jax.experimental import pallas as pl
from jax.experimental.pallas import tpu as pltpu
from jax.sharding import PartitionSpec as P

KVH = 8
HD = 128


def partner(shard, axis, bit):
    return lax.ppermute(shard, axis, [(i, i ^ 1 << bit) for i in range(lax.axis_size(axis))])


def rotate(values, position):
    half = values.shape[-1] // 2
    steps = jnp.arange(half, dtype=jnp.float32)
    freq = jnp.exp(-(2.0 * steps / (2 * half)) * jnp.log(jnp.float32(500000.0)))
    angle = position[:, None] * freq[None, :]
    cosine = jnp.cos(angle)[:, None, :]
    sine = jnp.sin(angle)[:, None, :]
    first = values[..., :half]
    second = values[..., half:]
    return jnp.concatenate(
        [first * cosine - second * sine, second * cosine + first * sine], axis=-1
    )


def add_product(piece, weights):
    return jnp.dot(piece, weights, preferred_element_type=jnp.float32)


def body(hidden_in, norm_gain, w_query, w_key, w_value, w_out, segment_ids):
    count = hidden_in.shape[0]
    as_float = hidden_in.astype(jnp.float32)
    full_rows, full_gain = (
        lax.all_gather(hidden_in, "weight", axis=1, tiled=True),
        lax.all_gather(norm_gain[None, :], "weight", axis=1, tiled=True),
    )
    rows_float = full_rows.astype(jnp.float32)
    mean_sq = jnp.mean(rows_float * rows_float, axis=1, keepdims=True)
    normed = (rows_float * lax.rsqrt(mean_sq + 1e-05) * full_gain.astype(jnp.float32)).astype(
        jnp.bfloat16
    )
    query_raw = jnp.dot(normed, w_query, preferred_element_type=jnp.float32)
    key_acc = jnp.dot(normed, w_key, preferred_element_type=jnp.float32)
    value_acc = jnp.dot(normed, w_value, preferred_element_type=jnp.float32)
    key_local = key_acc.astype(jnp.bfloat16)
    value_local = value_acc.astype(jnp.bfloat16)
    head_count = w_query.shape[1] // HD
    block_size = lax.axis_size("weight") // KVH
    my_index = lax.axis_index("weight")
    key_head, value_head = (key_local, value_local)
    for bit_number in range(block_size.bit_length() - 1):
        other_key, other_value = partner((key_head, value_head), "weight", bit_number)
        upper_half = my_index >> bit_number & 1 == 1
        key_head = jnp.where(
            upper_half,
            jnp.concatenate([other_key, key_head], axis=1),
            jnp.concatenate([key_head, other_key], axis=1),
        )
        value_head = jnp.where(
            upper_half,
            jnp.concatenate([other_value, value_head], axis=1),
            jnp.concatenate([value_head, other_value], axis=1),
        )
    index = jnp.arange(count, dtype=jnp.int32)
    same = segment_ids[:, None] == segment_ids[None, :]
    start_index = jnp.min(jnp.where(same, index[None, :], count), axis=1)
    position = (index - start_index).astype(jnp.float32)
    keep = same & (index[None, :] <= index[:, None])
    query = rotate(query_raw.reshape(count, head_count, HD), position).astype(jnp.bfloat16)
    key_rot = rotate(key_head.astype(jnp.float32).reshape(count, 1, HD), position).astype(
        jnp.bfloat16
    )[:, 0, :]
    scores = jnp.einsum(
        "thd,sd->hts", query, key_rot, preferred_element_type=jnp.float32
    ) / jnp.sqrt(jnp.float32(HD))
    scores = jnp.where(keep[None, :, :], scores, -jnp.inf)
    top = jnp.max(scores, axis=2, keepdims=True)
    probs = jnp.exp(scores - top)
    total = jnp.sum(probs, axis=2)
    weights = probs.astype(jnp.bfloat16)
    summed = jnp.einsum("hts,sd->thd", weights, value_head, preferred_element_type=jnp.float32)
    heads = (
        (summed / jnp.transpose(total)[:, :, None])
        .astype(jnp.bfloat16)
        .reshape(count, head_count * HD)
    )
    project = add_product(lax.all_gather(heads, "weight", axis=1, tiled=True), w_out)
    return (as_float + project).astype(jnp.bfloat16)


def dot(a, b):
    return jnp.dot(a, b, preferred_element_type=jnp.float32)


def spread(row, height):
    return jnp.broadcast_to(row, (height, row.shape[1])).T


def fused(
    n, hidden, gain, w_query, w_key, w_value, w_out, seg, out,
    buf, vq, vk, vv, vo, acc_q, acc_k, acc_v, acc_o, stats, rcol, cos_tab, sin_tab, bias,
    kv, kbuf, vbuf, load_sem, ring_send, ring_recv, sib_send, sib_recv,
    stat_send, stat_recv, kv_send, kv_recv,
):
    f32, bf16 = jnp.float32, jnp.bfloat16
    tokens, width = hidden.shape
    rows = tokens // 2
    piece = rows // 2
    heads = width // HD
    half = HD // 2
    chips = n // 2
    zs = chips // 2
    me = lax.axis_index("weight")
    core = me % 2
    chip = me // 2
    pos = (chip // 2) * (1 - chip % 2) + (2 * zs - 1 - chip // 2) * (chip % 2)
    sib = me + 1 - 2 * core

    def chip_at(place):
        place = (place + 2 * chips) % chips
        y = place // zs
        z = place * (1 - y) + (2 * zs - 1 - place) * y
        return z * 2 + y

    def at(place):
        return chip_at(place) * 2 + core

    peers = (at(pos + 1), at(pos - 1))

    def remote(src, dst, send, recv, target):
        return pltpu.make_async_remote_copy(
            src_ref=src, dst_ref=dst, send_sem=send, recv_sem=recv,
            device_id={"weight": target}, device_id_type=pl.DeviceIdType.MESH,
        )

    def ring(way, stage, step, part):
        owner = at(pos - step) if way == 0 else at(pos + step)
        ref = buf.at[stage, owner, pl.ds(part * piece, piece)]
        return remote(
            ref, ref, ring_send.at[way, stage, step, part], ring_recv.at[way, stage, step, part],
            peers[way],
        )

    def arrival(way, stage, step, part):
        owner = at(pos - step - 1) if way == 0 else at(pos + step + 1)
        ref = buf.at[stage, owner, pl.ds(part * piece, piece)]
        return remote(
            ref, ref, ring_send.at[way, stage, step, part], ring_recv.at[way, stage, step, part],
            peers[way],
        )

    def share(stage, slot, place, own):
        owner = chip_at(place) * 2 + (core if own else 1 - core)
        ref = buf.at[stage, owner]
        return remote(ref, ref, sib_send.at[stage, slot], sib_recv.at[stage, slot], sib)

    def send_own(stage):
        for part in range(2):
            for way in range(2):
                ring(way, stage, 0, part).start()
        share(stage, 0, pos, True).start()

    def kv_copy(stage, side):
        ref = kv.at[stage, side]
        return remote(ref, ref, kv_send.at[stage], kv_recv.at[stage], sib)

    own_x = [
        pltpu.make_async_copy(
            hidden.at[pl.ds(stage * rows, rows)], buf.at[stage, me], load_sem.at[4 + stage]
        )
        for stage in range(2)
    ]
    for copy in own_x:
        copy.start()
    loads = [
        pltpu.make_async_copy(src, dst, load_sem.at[i])
        for i, (src, dst) in enumerate(
            ((w_query, vq), (w_key, vk), (w_value, vv), (w_out, vo))
        )
    ]
    for copy in loads:
        copy.start()

    barrier = pltpu.get_barrier_semaphore()

    def greet(i, carry):
        pl.semaphore_signal(
            barrier, inc=1, device_id={"weight": (me + i) % n},
            device_id_type=pl.DeviceIdType.MESH,
        )
        return carry

    lax.fori_loop(1, n, greet, 0)
    for copy in own_x:
        copy.wait()
    pl.semaphore_wait(barrier, n - 1)
    send_own(0)

    squares = []
    for stage in range(2):
        values = buf[stage, me].astype(f32)
        squares.append(jnp.sum(values * values, axis=1, keepdims=True))
    column = jnp.broadcast_to(jnp.concatenate(squares, axis=0), (tokens, 128))
    upper = lax.broadcasted_iota(jnp.int32, (8, width), 0) < 4
    own_gain = jnp.broadcast_to(gain[...].astype(f32), (8, width))
    stats[me] = jnp.where(upper, column.T[0:8], own_gain)

    def stat_copy(i, owner):
        ref = stats.at[owner]
        return remote(ref, ref, stat_send.at[i], stat_recv.at[i], (me + i) % n)

    def send_stat(i, carry):
        stat_copy(i, me).start()
        return carry

    lax.fori_loop(1, n, send_stat, 0)

    seg_row = seg[...].astype(f32)
    padded = jnp.concatenate([jnp.full((1, 128), -1.0, f32), seg_row], axis=1)
    seg_col = spread(seg_row, 128)
    window = rows + 128
    lane = lax.broadcasted_iota(jnp.int32, (rows, HD), 1)
    freq = jnp.exp(
        -(2.0 * (lane % half).astype(f32) / HD) * jnp.log(jnp.float32(500000.0))
    )
    for stage in range(2):
        first = stage * rows
        col = seg_col[first:first + rows]
        same = jnp.concatenate([col] * (window // 128), axis=1) == padded[:, first:first + window]
        key_at = lax.broadcasted_iota(jnp.int32, (rows, window), 1) + (first - 128)
        query_at = lax.broadcasted_iota(jnp.int32, (rows, window), 0) + first
        bias[stage] = jnp.where(same & (key_at <= query_at), 0.0, -jnp.inf)
        start = jnp.min(
            jnp.where(same, key_at.astype(f32), jnp.float32(tokens)), axis=1, keepdims=True
        )
        token = (lax.broadcasted_iota(jnp.int32, (rows, HD), 0) + first).astype(f32)
        angle = (token - start) * freq
        cos_tab[stage] = jnp.cos(angle)
        sine = jnp.sin(angle)
        sin_tab[stage] = jnp.where(lane < half, -sine, sine)
    acc_q[...] = jnp.zeros_like(acc_q)
    acc_k[...] = jnp.zeros_like(acc_k)
    acc_v[...] = jnp.zeros_like(acc_v)
    acc_o[...] = jnp.zeros_like(acc_o)
    kbuf[0:128] = jnp.zeros((128, HD), bf16)
    vbuf[0:128] = jnp.zeros((128, HD), bf16)

    def wait_stat(i, carry):
        stat_copy(i, (me - i + n) % n).wait_recv()
        return carry

    lax.fori_loop(1, n, wait_stat, 0)
    total = jnp.sum(stats[...], axis=0)[0:1]
    scale = lax.rsqrt(total / jnp.float32(n * width) + 1e-05)
    rcol[...] = spread(scale, 128)
    for copy in loads:
        copy.wait()

    def turn(values, stage):
        other = jnp.concatenate([values[:, half:], values[:, :half]], axis=1)
        return (values * cos_tab[stage] + other * sin_tab[stage]).astype(bf16)

    def project(stage, owner):
        scale_rows = rcol[pl.ds(pl.multiple_of(stage * rows, rows), rows)]
        wide = jnp.concatenate([scale_rows] * (width // 128), axis=1)
        block = (
            buf[stage, owner].astype(f32) * wide * stats[owner, 4:5]
        ).astype(bf16)
        depth = pl.ds(pl.multiple_of(owner * width, width), width)
        acc_q[stage] += dot(block, vq[depth])
        acc_k[stage] += dot(block, vk[depth])
        acc_v[stage] += dot(block, vv[depth])

    def combine(stage, owner):
        depth = pl.ds(pl.multiple_of(owner * width, width), width)
        acc_o[stage - 2] += dot(buf[stage, owner], vo[depth])

    def use(stage, owner):
        @pl.when(stage < 2)
        def _():
            project(stage, owner)

        @pl.when(stage >= 2)
        def _():
            combine(stage, owner)

    def attend(stage):
        kv_copy(stage, 1 - core).wait_recv()
        low, high = kv[stage, 0], kv[stage, 1]
        keys = jnp.concatenate([low[:, :half], high[:, :half]], axis=1)
        values = jnp.concatenate([low[:, half:], high[:, half:]], axis=1)
        here = pl.ds(pl.multiple_of(stage * rows + 128, 128), rows)
        kbuf[here] = turn(keys.astype(f32), stage)
        vbuf[here] = values
        near = pl.ds(pl.multiple_of(stage * rows, 128), window)
        key_win = kbuf[near]
        value_win = vbuf[near]
        for head in range(heads):
            cols = slice(head * HD, head * HD + HD)
            query = turn(acc_q[stage, :, cols], stage)
            scores = lax.dot_general(
                query, key_win, (((1,), (1,)), ((), ())), preferred_element_type=f32
            ) / jnp.sqrt(jnp.float32(HD)) + bias[stage]
            probs = jnp.exp(scores - jnp.max(scores, axis=1, keepdims=True))
            mass = jnp.sum(probs, axis=1, keepdims=True)
            buf[stage + 2, me, :, cols] = (dot(probs.astype(bf16), value_win) / mass).astype(bf16)

    def step_body(t, carry):
        stage = t // 4
        step = t % 4

        @pl.when((step == 3) & (stage < 3))
        def _():
            send_own(stage + 1)

        for part in range(2):
            for way in range(2):
                @pl.when((step < 3) | (part == way))
                def _():
                    arrival(way, stage, step, part).wait_recv()

                @pl.when((step < 2) | ((step == 2) & (part == way)))
                def _():
                    ring(way, stage, step + 1, part).start()

        @pl.when(step < 3)
        def _():
            share(stage, step + 1, pos - step - 1, True).start()
            share(stage, step + 4, pos + step + 1, True).start()

        @pl.when(step == 3)
        def _():
            share(stage, 7, pos + 4, True).start()

        @pl.when((step == 0) & ((stage == 1) | (stage == 2)))
        def _():
            attend(stage - 1)

        def unit(u, carry):
            last = u // 2
            left = u % 2
            right = 1 - left - last
            place = pos - step * right + step * left + 4 * last
            slot = step * right + (step + 3) * left + 7 * last

            @pl.when((u == 0) | ((u == 1) & (step > 0)) | ((u == 2) & (step == 3)))
            def _():
                share(stage, slot, place, False).wait_recv()
                first = chip_at(place) * 2

                def one(k, carry):
                    use(stage, first + k)
                    return carry

                lax.fori_loop(0, 2, one, 0)

            return carry

        lax.fori_loop(0, 3, unit, 0)

        @pl.when((step == 3) & (stage < 2))
        def _():
            kv[stage, core] = jnp.concatenate(
                [acc_k[stage].astype(bf16), acc_v[stage].astype(bf16)], axis=1
            )
            kv_copy(stage, core).start()

        return carry

    lax.fori_loop(0, 16, step_body, 0)

    for stage in range(2):
        out[stage * rows:(stage + 1) * rows] = (
            buf[stage, me].astype(f32) + acc_o[stage]
        ).astype(bf16)

    def finish(stage, carry):
        for way in range(2):
            for step in range(4):
                for part in range(2):
                    if step < 3 or part == way:
                        ring(way, stage, step, part).wait_send()
        for slot, away in enumerate((0, -1, -2, -3, 1, 2, 3, 4)):
            share(stage, slot, pos + away, True).wait_send()
        return carry

    lax.fori_loop(0, 4, finish, 0)
    for stage in range(2):
        kv_copy(stage, core).wait_send()

    def left(i, carry):
        stat_copy(i, me).wait_send()
        return carry

    lax.fori_loop(1, n, left, 0)


def ring_body(hidden_in, norm_gain, w_query, w_key, w_value, w_out, segment_ids):
    n = lax.axis_size("weight")
    tokens, width = hidden_in.shape
    depth = w_query.shape[0]
    rows = tokens // 2
    kvw = w_key.shape[1]
    f32, bf16 = jnp.float32, jnp.bfloat16
    anywhere = pl.BlockSpec(memory_space=pl.ANY)
    vmem = pl.BlockSpec(memory_space=pltpu.VMEM)
    dma = pltpu.SemaphoreType.DMA
    return pl.pallas_call(
        functools.partial(fused, n),
        out_shape=jax.ShapeDtypeStruct((tokens, width), bf16),
        in_specs=[anywhere, vmem, anywhere, anywhere, anywhere, anywhere, vmem],
        out_specs=vmem,
        scratch_shapes=[
            pltpu.VMEM((4, n, rows, width), bf16),
            pltpu.VMEM(w_query.shape, bf16),
            pltpu.VMEM(w_key.shape, bf16),
            pltpu.VMEM(w_value.shape, bf16),
            pltpu.VMEM(w_out.shape, bf16),
            pltpu.VMEM((2, rows, w_query.shape[1]), f32),
            pltpu.VMEM((2, rows, kvw), f32),
            pltpu.VMEM((2, rows, kvw), f32),
            pltpu.VMEM((2, rows, width), f32),
            pltpu.VMEM((n, 8, tokens), f32),
            pltpu.VMEM((tokens, 128), f32),
            pltpu.VMEM((2, rows, HD), f32),
            pltpu.VMEM((2, rows, HD), f32),
            pltpu.VMEM((2, rows, rows + 128), f32),
            pltpu.VMEM((2, 2, rows, 2 * kvw), bf16),
            pltpu.VMEM((tokens + 128, HD), bf16),
            pltpu.VMEM((tokens + 128, HD), bf16),
            dma((6,)),
            dma((2, 4, 4, 2)),
            dma((2, 4, 4, 2)),
            dma((4, 8)),
            dma((4, 8)),
            dma((n,)),
            dma((n,)),
            dma((2,)),
            dma((2,)),
        ],
        compiler_params=pltpu.CompilerParams(
            collective_id=0, has_side_effects=True, vmem_limit_bytes=56 * 1024 * 1024
        ),
    )(
        hidden_in, norm_gain[None, :], w_query, w_key, w_value, w_out, segment_ids[None, :]
    )


def solution(mesh):
    placed = (
        P("group", "weight"),
        P("weight"),
        P(None, "weight"),
        P(None, "weight"),
        P(None, "weight"),
        P(None, "weight"),
        P("group"),
    )
    chosen = ring_body if mesh.shape["weight"] == 2 * KVH else body
    return jax.shard_map(
        chosen, mesh=mesh, in_specs=placed, out_specs=P("group", "weight"), check_vma=False
    )
```

```python
import functools

import jax
import jax.numpy as jnp
from jax import lax
from jax.experimental import pallas as pl
from jax.experimental.pallas import tpu as pltpu
from jax.sharding import PartitionSpec as P

KVH = 8
PARTS = 4
HD = 128


def partner(shard, axis, bit):
    return lax.ppermute(shard, axis, [(i, i ^ 1 << bit) for i in range(lax.axis_size(axis))])


def rotate(values, position):
    half = values.shape[-1] // 2
    steps = jnp.arange(half, dtype=jnp.float32)
    freq = jnp.exp(-(2.0 * steps / (2 * half)) * jnp.log(jnp.float32(500000.0)))
    angle = position[:, None] * freq[None, :]
    cosine = jnp.cos(angle)[:, None, :]
    sine = jnp.sin(angle)[:, None, :]
    first = values[..., :half]
    second = values[..., half:]
    return jnp.concatenate(
        [first * cosine - second * sine, second * cosine + first * sine], axis=-1
    )


def add_product(piece, weights):
    return jnp.dot(piece, weights, preferred_element_type=jnp.float32)


def body(hidden_in, norm_gain, w_query, w_key, w_value, w_out, segment_ids):
    count = hidden_in.shape[0]
    as_float = hidden_in.astype(jnp.float32)
    full_rows, full_gain = (
        lax.all_gather(hidden_in, "weight", axis=1, tiled=True),
        lax.all_gather(norm_gain[None, :], "weight", axis=1, tiled=True),
    )
    rows_float = full_rows.astype(jnp.float32)
    mean_sq = jnp.mean(rows_float * rows_float, axis=1, keepdims=True)
    normed = (rows_float * lax.rsqrt(mean_sq + 1e-05) * full_gain.astype(jnp.float32)).astype(
        jnp.bfloat16
    )
    query_raw = jnp.dot(normed, w_query, preferred_element_type=jnp.float32)
    key_acc = jnp.dot(normed, w_key, preferred_element_type=jnp.float32)
    value_acc = jnp.dot(normed, w_value, preferred_element_type=jnp.float32)
    key_local = key_acc.astype(jnp.bfloat16)
    value_local = value_acc.astype(jnp.bfloat16)
    head_count = w_query.shape[1] // HD
    block_size = lax.axis_size("weight") // KVH
    my_index = lax.axis_index("weight")
    key_head, value_head = (key_local, value_local)
    for bit_number in range(block_size.bit_length() - 1):
        other_key, other_value = partner((key_head, value_head), "weight", bit_number)
        upper_half = my_index >> bit_number & 1 == 1
        key_head = jnp.where(
            upper_half,
            jnp.concatenate([other_key, key_head], axis=1),
            jnp.concatenate([key_head, other_key], axis=1),
        )
        value_head = jnp.where(
            upper_half,
            jnp.concatenate([other_value, value_head], axis=1),
            jnp.concatenate([value_head, other_value], axis=1),
        )
    index = jnp.arange(count, dtype=jnp.int32)
    same = segment_ids[:, None] == segment_ids[None, :]
    start_index = jnp.min(jnp.where(same, index[None, :], count), axis=1)
    position = (index - start_index).astype(jnp.float32)
    keep = same & (index[None, :] <= index[:, None])
    query = rotate(query_raw.reshape(count, head_count, HD), position).astype(jnp.bfloat16)
    key_rot = rotate(key_head.astype(jnp.float32).reshape(count, 1, HD), position).astype(
        jnp.bfloat16
    )[:, 0, :]
    scores = jnp.einsum(
        "thd,sd->hts", query, key_rot, preferred_element_type=jnp.float32
    ) / jnp.sqrt(jnp.float32(HD))
    scores = jnp.where(keep[None, :, :], scores, -jnp.inf)
    top = jnp.max(scores, axis=2, keepdims=True)
    probs = jnp.exp(scores - top)
    total = jnp.sum(probs, axis=2)
    weights = probs.astype(jnp.bfloat16)
    summed = jnp.einsum("hts,sd->thd", weights, value_head, preferred_element_type=jnp.float32)
    heads = (
        (summed / jnp.transpose(total)[:, :, None])
        .astype(jnp.bfloat16)
        .reshape(count, head_count * HD)
    )
    project = add_product(lax.all_gather(heads, "weight", axis=1, tiled=True), w_out)
    return (as_float + project).astype(jnp.bfloat16)


def dot(a, b):
    return jnp.dot(a, b, preferred_element_type=jnp.float32)


def dot_t(a, b):
    return lax.dot_general(
        a, b, (((1,), (1,)), ((), ())), preferred_element_type=jnp.float32
    )


def spread(row, height):
    return jnp.broadcast_to(row, (height, row.shape[1])).T


def fused(
    n, hidden, gain, w_query, w_key, w_value, w_out, seg, out,
    buf, vq, vkv, vo, acc_q, acc_kv, acc_o, stats, rcol, seg_row, seg_col, cos_tab, sin_tab, bias,
    kv, kbuf, vbuf, load_sem, ring_send, ring_recv, sib_send, sib_recv,
    stat_send, stat_recv, kv_send, kv_recv,
):
    f32, bf16 = jnp.float32, jnp.bfloat16
    tokens, width = hidden.shape
    rows = tokens // 2
    piece = rows // PARTS
    heads = width // HD
    half = HD // 2
    kvw = w_key.shape[0]
    window = rows + 128
    chips = n // 2
    zs = chips // 2
    me = lax.axis_index("weight")
    core = me % 2
    chip = me // 2
    pos = (chip // 2) * (1 - chip % 2) + (2 * zs - 1 - chip // 2) * (chip % 2)
    sib = me + 1 - 2 * core

    def chip_at(place):
        place = (place + 2 * chips) % chips
        y = place // zs
        z = place * (1 - y) + (2 * zs - 1 - place) * y
        return z * 2 + y

    def at(place):
        return chip_at(place) * 2 + core

    peers = (at(pos + 1), at(pos - 1))

    def remote(src, dst, send, recv, target):
        return pltpu.make_async_remote_copy(
            src_ref=src, dst_ref=dst, send_sem=send, recv_sem=recv,
            device_id={"weight": target}, device_id_type=pl.DeviceIdType.MESH,
        )

    def ring(way, stage, step, part):
        owner = at(pos - step) if way == 0 else at(pos + step)
        ref = buf.at[stage, owner, pl.ds(part * piece, piece)]
        return remote(
            ref, ref, ring_send.at[way, stage, step, part], ring_recv.at[way, stage, step, part],
            peers[way],
        )

    def arrival(way, stage, step, part):
        owner = at(pos - step - 1) if way == 0 else at(pos + step + 1)
        ref = buf.at[stage, owner, pl.ds(part * piece, piece)]
        return remote(
            ref, ref, ring_send.at[way, stage, step, part], ring_recv.at[way, stage, step, part],
            peers[way],
        )

    def share(stage, slot, place, own):
        owner = chip_at(place) * 2 + (core if own else 1 - core)
        ref = buf.at[stage, owner]
        return remote(ref, ref, sib_send.at[stage, slot], sib_recv.at[stage, slot], sib)

    def send_own(stage):
        for part in range(PARTS):
            for way in range(2):
                ring(way, stage, 0, part).start()
        share(stage, 0, pos, True).start()

    def kv_copy(stage, side):
        ref = kv.at[stage, side]
        return remote(ref, ref, kv_send.at[stage], kv_recv.at[stage], sib)

    own_x = [
        pltpu.make_async_copy(
            hidden.at[pl.ds(stage * rows, rows)], buf.at[stage, me], load_sem.at[4 + stage]
        )
        for stage in range(2)
    ]
    for copy in own_x:
        copy.start()
    loads = [
        pltpu.make_async_copy(src, dst, load_sem.at[i])
        for i, (src, dst) in enumerate(
            (
                (w_query, vq),
                (w_key, vkv.at[pl.ds(0, kvw)]),
                (w_value, vkv.at[pl.ds(kvw, kvw)]),
                (w_out, vo),
            )
        )
    ]
    for copy in loads:
        copy.start()

    barrier = pltpu.get_barrier_semaphore()

    def greet(i, carry):
        pl.semaphore_signal(
            barrier, inc=1, device_id={"weight": (me + 2 * i) % n},
            device_id_type=pl.DeviceIdType.MESH,
        )
        return carry

    lax.fori_loop(1, chips, greet, 0)
    pl.semaphore_signal(
        barrier, inc=1, device_id={"weight": sib}, device_id_type=pl.DeviceIdType.MESH
    )
    acc_q[...] = jnp.zeros_like(acc_q)
    acc_kv[...] = jnp.zeros_like(acc_kv)
    acc_o[...] = jnp.zeros_like(acc_o)
    kbuf[0:128] = jnp.zeros((128, HD), bf16)
    vbuf[0:128] = jnp.zeros((128, HD), bf16)
    ids = seg[...].astype(f32)
    seg_row[...] = jnp.broadcast_to(
        jnp.concatenate([jnp.full((1, 128), -1.0, f32), ids], axis=1), seg_row.shape
    )
    seg_col[...] = spread(ids, 128)
    for copy in own_x:
        copy.wait()

    groups = tokens // 128
    lines = []
    for stage in range(2):
        values = buf[stage, me].astype(f32)
        sums = jnp.sum(values * values, axis=1, keepdims=True)
        across = jnp.broadcast_to(sums, (rows, 128)).T[0:1]
        lines += [across[:, i * 128:(i + 1) * 128] for i in range(rows // 128)]
    own_gain = gain[...].astype(f32).reshape(1, width)
    lines += [own_gain[:, i * 128:(i + 1) * 128] for i in range(width // 128)]
    stats[core, chip] = jnp.concatenate(lines, axis=0)

    def stat_copy(i, owner):
        ref = stats.at[core, owner]
        return remote(ref, ref, stat_send.at[i], stat_recv.at[i], (me + 2 * i) % n)

    def stat_share(side):
        ref = stats.at[side]
        return remote(ref, ref, stat_send.at[0], stat_recv.at[0], sib)

    def send_stat(i, carry):
        stat_copy(i, chip).start()
        return carry

    pl.semaphore_wait(barrier, chips)
    lax.fori_loop(1, chips, send_stat, 0)
    send_own(0)

    def prepare():
        def wait_stat(i, carry):
            stat_copy(i, (chip - i + chips) % chips).wait_recv()
            return carry

        lax.fori_loop(1, chips, wait_stat, 0)
        stat_share(core).start()
        stat_share(1 - core).wait_recv()
        total = jnp.sum(stats[0] + stats[1], axis=0)
        scale = lax.rsqrt(total / jnp.float32(n * width) + 1e-05)
        for i in range(groups):
            rcol[i * 128:(i + 1) * 128] = spread(scale[i:i + 1], 128)
        for copy in loads:
            copy.wait()

    def tables(stage):
        first = stage * rows
        lane = lax.broadcasted_iota(jnp.int32, (rows, HD), 1)
        freq = jnp.exp(
            -(2.0 * (lane % half).astype(f32) / HD) * jnp.log(jnp.float32(500000.0))
        )
        col = seg_col[pl.ds(pl.multiple_of(first, rows), rows)]
        row = seg_row[0:1, pl.ds(pl.multiple_of(first, 128), window)]
        same = jnp.concatenate([col] * (window // 128), axis=1) == row
        key_at = lax.broadcasted_iota(jnp.int32, (rows, window), 1) + (first - 128)
        query_at = lax.broadcasted_iota(jnp.int32, (rows, window), 0) + first
        bias[stage] = jnp.where(same & (key_at <= query_at), 0.0, -jnp.inf)
        start = jnp.min(
            jnp.where(same, key_at.astype(f32), jnp.float32(tokens)), axis=1, keepdims=True
        )
        token = (lax.broadcasted_iota(jnp.int32, (rows, HD), 0) + first).astype(f32)
        angle = (token - start) * freq
        cos_tab[stage] = jnp.cos(angle)
        sine = jnp.sin(angle)
        sin_tab[stage] = jnp.where(lane < half, -sine, sine)

    def turn(values, stage):
        other = jnp.concatenate([values[:, half:], values[:, :half]], axis=1)
        return (values * cos_tab[stage] + other * sin_tab[stage]).astype(bf16)

    def project(stage, owner):
        scale_rows = rcol[pl.ds(pl.multiple_of(stage * rows, rows), rows)]
        wide = jnp.concatenate([scale_rows] * (width // 128), axis=1)
        tile = stats[owner % 2, owner // 2]
        gains = jnp.concatenate(
            [tile[groups + i:groups + i + 1] for i in range(width // 128)], axis=1
        )
        block = (buf[stage, owner].astype(f32) * wide * gains).astype(bf16)
        depth = pl.ds(pl.multiple_of(owner * width, width), width)
        acc_q[stage] += dot(block, vq[depth])
        acc_kv[stage] += dot_t(block, vkv[:, depth])

    def combine(stage, owner):
        depth = pl.ds(pl.multiple_of(owner * width, width), width)
        acc_o[stage - 2] += dot(buf[stage, owner], vo[depth])

    def use(stage, owner):
        @pl.when(stage < 2)
        def _():
            project(stage, owner)

        @pl.when(stage >= 2)
        def _():
            combine(stage, owner)

    def keys_of(stage):
        kv_copy(stage, 1 - core).wait_recv()
        low, high = kv[stage, 0], kv[stage, 1]
        keys = jnp.concatenate([low[:, :half], high[:, :half]], axis=1)
        values = jnp.concatenate([low[:, half:], high[:, half:]], axis=1)
        here = pl.ds(pl.multiple_of(stage * rows + 128, 128), rows)
        kbuf[here] = turn(keys.astype(f32), stage)
        vbuf[here] = values

    def attend(stage, head):
        near = pl.ds(pl.multiple_of(stage * rows, 128), window)
        key_win = kbuf[near]
        value_win = vbuf[near]
        cols = pl.ds(pl.multiple_of(head * HD, HD), HD)
        query = turn(acc_q[stage, :, cols], stage)
        scores = dot_t(query, key_win) / jnp.sqrt(jnp.float32(HD)) + bias[stage]
        probs = jnp.exp(scores - jnp.max(scores, axis=1, keepdims=True))
        mass = jnp.sum(probs, axis=1, keepdims=True)
        buf[stage + 2, me, :, cols] = (dot(probs.astype(bf16), value_win) / mass).astype(bf16)

    def step_body(t, carry):
        stage = t // 4
        step = t % 4

        @pl.when((step == 3) & (stage < 3))
        def _():
            send_own(stage + 1)

        @pl.when(step < 3)
        def _():
            for part in range(PARTS):
                for way in range(2):
                    arrival(way, stage, step, part).wait_recv()

                    @pl.when((step < 2) | (part % 2 == way))
                    def _():
                        ring(way, stage, step + 1, part).start()

            share(stage, step + 1, pos - step - 1, True).start()
            share(stage, step + 4, pos + step + 1, True).start()

        @pl.when(t == 0)
        def _():
            prepare()

        @pl.when((t == 1) | (t == 2))
        def _():
            tables(t - 1)

        @pl.when((step == 0) & ((stage == 1) | (stage == 2)))
        def _():
            keys_of(stage - 1)

        @pl.when((step < 2) & ((stage == 1) | (stage == 2)))
        def _():
            def one_head(head, carry):
                attend(stage - 1, head)
                return carry

            lax.fori_loop(step * (heads // 2), (step + 1) * (heads // 2), one_head, 0)

        def unit(u, carry):
            last = u // 2
            left = u % 2
            right = 1 - left - last
            place = pos - step * right + step * left + 4 * last
            slot = step * right + (step + 3) * left + 7 * last

            @pl.when((u == 0) | ((u == 1) & (step > 0)) | ((u == 2) & (step == 3)))
            def _():
                @pl.when(u == 2)
                def _():
                    for part in range(PARTS):
                        arrival(part % 2, stage, 3, part).wait_recv()

                    share(stage, 7, pos + 4, True).start()

                share(stage, slot, place, False).wait_recv()
                first = chip_at(place) * 2

                def one(k, carry):
                    use(stage, first + k)
                    return carry

                lax.fori_loop(0, 2, one, 0)

            return carry

        lax.fori_loop(0, 3, unit, 0)

        @pl.when((step == 3) & (stage < 2))
        def _():
            kv[stage, core] = acc_kv[stage].astype(bf16)
            kv_copy(stage, core).start()

        return carry

    lax.fori_loop(0, 16, step_body, 0)

    for stage in range(2):
        out[stage * rows:(stage + 1) * rows] = (
            buf[stage, me].astype(f32) + acc_o[stage]
        ).astype(bf16)

    def finish(stage, carry):
        for way in range(2):
            for step in range(4):
                for part in range(PARTS):
                    if step < 3 or part % 2 == way:
                        ring(way, stage, step, part).wait_send()
        for slot, away in enumerate((0, -1, -2, -3, 1, 2, 3, 4)):
            share(stage, slot, pos + away, True).wait_send()
        return carry

    lax.fori_loop(0, 4, finish, 0)
    for stage in range(2):
        kv_copy(stage, core).wait_send()

    def left(i, carry):
        stat_copy(i, chip).wait_send()
        return carry

    lax.fori_loop(1, chips, left, 0)
    stat_share(core).wait_send()


def ring_body(hidden_in, norm_gain, w_query, w_key, w_value, w_out, segment_ids):
    n = lax.axis_size("weight")
    tokens, width = hidden_in.shape
    depth = w_query.shape[0]
    rows = tokens // 2
    kvw = w_key.shape[1]
    f32, bf16 = jnp.float32, jnp.bfloat16
    anywhere = pl.BlockSpec(memory_space=pl.ANY)
    vmem = pl.BlockSpec(memory_space=pltpu.VMEM)
    dma = pltpu.SemaphoreType.DMA
    return pl.pallas_call(
        functools.partial(fused, n),
        out_shape=jax.ShapeDtypeStruct((tokens, width), bf16),
        in_specs=[anywhere, vmem, anywhere, anywhere, anywhere, anywhere, vmem],
        out_specs=vmem,
        scratch_shapes=[
            pltpu.VMEM((4, n, rows, width), bf16),
            pltpu.VMEM(w_query.shape, bf16),
            pltpu.VMEM((2 * kvw, depth), bf16),
            pltpu.VMEM(w_out.shape, bf16),
            pltpu.VMEM((2, rows, w_query.shape[1]), f32),
            pltpu.VMEM((2, rows, 2 * kvw), f32),
            pltpu.VMEM((2, rows, width), f32),
            pltpu.VMEM((2, n // 2, (tokens + width) // 128, 128), f32),
            pltpu.VMEM((tokens, 128), f32),
            pltpu.VMEM((8, tokens + 128), f32),
            pltpu.VMEM((tokens, 128), f32),
            pltpu.VMEM((2, rows, HD), f32),
            pltpu.VMEM((2, rows, HD), f32),
            pltpu.VMEM((2, rows, rows + 128), f32),
            pltpu.VMEM((2, 2, rows, 2 * kvw), bf16),
            pltpu.VMEM((tokens + 128, HD), bf16),
            pltpu.VMEM((tokens + 128, HD), bf16),
            dma((6,)),
            dma((2, 4, 4, PARTS)),
            dma((2, 4, 4, PARTS)),
            dma((4, 8)),
            dma((4, 8)),
            dma((n // 2,)),
            dma((n // 2,)),
            dma((2,)),
            dma((2,)),
        ],
        compiler_params=pltpu.CompilerParams(
            collective_id=0, has_side_effects=True, vmem_limit_bytes=56 * 1024 * 1024
        ),
    )(
        hidden_in, norm_gain, w_query, w_key.T, w_value.T, w_out, segment_ids[None, :]
    )


def solution(mesh):
    placed = (
        P("group", "weight"),
        P("weight"),
        P(None, "weight"),
        P(None, "weight"),
        P(None, "weight"),
        P(None, "weight"),
        P("group"),
    )
    chosen = ring_body if mesh.shape["weight"] == 2 * KVH else body
    return jax.shard_map(
        chosen, mesh=mesh, in_specs=placed, out_specs=P("group", "weight"), check_vma=False
    )
```

```python
import functools

import jax
import jax.numpy as jnp
from jax import lax
from jax.experimental import pallas as pl
from jax.experimental.pallas import tpu as pltpu
from jax.sharding import PartitionSpec as P

KVH = 8
PARTS = 4
HD = 128


def partner(shard, axis, bit):
    return lax.ppermute(shard, axis, [(i, i ^ 1 << bit) for i in range(lax.axis_size(axis))])


def rotate(values, position):
    half = values.shape[-1] // 2
    steps = jnp.arange(half, dtype=jnp.float32)
    freq = jnp.exp(-(2.0 * steps / (2 * half)) * jnp.log(jnp.float32(500000.0)))
    angle = position[:, None] * freq[None, :]
    cosine = jnp.cos(angle)[:, None, :]
    sine = jnp.sin(angle)[:, None, :]
    first = values[..., :half]
    second = values[..., half:]
    return jnp.concatenate(
        [first * cosine - second * sine, second * cosine + first * sine], axis=-1
    )


def add_product(piece, weights):
    return jnp.dot(piece, weights, preferred_element_type=jnp.float32)


def body(hidden_in, norm_gain, w_query, w_key, w_value, w_out, segment_ids):
    count = hidden_in.shape[0]
    as_float = hidden_in.astype(jnp.float32)
    full_rows, full_gain = (
        lax.all_gather(hidden_in, "weight", axis=1, tiled=True),
        lax.all_gather(norm_gain[None, :], "weight", axis=1, tiled=True),
    )
    rows_float = full_rows.astype(jnp.float32)
    mean_sq = jnp.mean(rows_float * rows_float, axis=1, keepdims=True)
    normed = (rows_float * lax.rsqrt(mean_sq + 1e-05) * full_gain.astype(jnp.float32)).astype(
        jnp.bfloat16
    )
    query_raw = jnp.dot(normed, w_query, preferred_element_type=jnp.float32)
    key_acc = jnp.dot(normed, w_key, preferred_element_type=jnp.float32)
    value_acc = jnp.dot(normed, w_value, preferred_element_type=jnp.float32)
    key_local = key_acc.astype(jnp.bfloat16)
    value_local = value_acc.astype(jnp.bfloat16)
    head_count = w_query.shape[1] // HD
    block_size = lax.axis_size("weight") // KVH
    my_index = lax.axis_index("weight")
    key_head, value_head = (key_local, value_local)
    for bit_number in range(block_size.bit_length() - 1):
        other_key, other_value = partner((key_head, value_head), "weight", bit_number)
        upper_half = my_index >> bit_number & 1 == 1
        key_head = jnp.where(
            upper_half,
            jnp.concatenate([other_key, key_head], axis=1),
            jnp.concatenate([key_head, other_key], axis=1),
        )
        value_head = jnp.where(
            upper_half,
            jnp.concatenate([other_value, value_head], axis=1),
            jnp.concatenate([value_head, other_value], axis=1),
        )
    index = jnp.arange(count, dtype=jnp.int32)
    same = segment_ids[:, None] == segment_ids[None, :]
    start_index = jnp.min(jnp.where(same, index[None, :], count), axis=1)
    position = (index - start_index).astype(jnp.float32)
    keep = same & (index[None, :] <= index[:, None])
    query = rotate(query_raw.reshape(count, head_count, HD), position).astype(jnp.bfloat16)
    key_rot = rotate(key_head.astype(jnp.float32).reshape(count, 1, HD), position).astype(
        jnp.bfloat16
    )[:, 0, :]
    scores = jnp.einsum(
        "thd,sd->hts", query, key_rot, preferred_element_type=jnp.float32
    ) / jnp.sqrt(jnp.float32(HD))
    scores = jnp.where(keep[None, :, :], scores, -jnp.inf)
    top = jnp.max(scores, axis=2, keepdims=True)
    probs = jnp.exp(scores - top)
    total = jnp.sum(probs, axis=2)
    weights = probs.astype(jnp.bfloat16)
    summed = jnp.einsum("hts,sd->thd", weights, value_head, preferred_element_type=jnp.float32)
    heads = (
        (summed / jnp.transpose(total)[:, :, None])
        .astype(jnp.bfloat16)
        .reshape(count, head_count * HD)
    )
    project = add_product(lax.all_gather(heads, "weight", axis=1, tiled=True), w_out)
    return (as_float + project).astype(jnp.bfloat16)


def dot(a, b):
    return jnp.dot(a, b, preferred_element_type=jnp.float32)


def dot_t(a, b):
    return lax.dot_general(
        a, b, (((1,), (1,)), ((), ())), preferred_element_type=jnp.float32
    )


def spread(row, height):
    return jnp.broadcast_to(row, (height, row.shape[1])).T


def fused(
    n, hidden, gain, w_query, w_key, w_value, w_out, seg, out,
    buf, vq, vkv, vo, acc_q, acc_kv, acc_o, stats, rcol, seg_row, seg_col, cos_tab, sin_tab, bias,
    kv, kbuf, vbuf, load_sem, ring_send, ring_recv, sib_send, sib_recv,
    stat_send, stat_recv, kv_send, kv_recv,
):
    f32, bf16 = jnp.float32, jnp.bfloat16
    tokens, width = hidden.shape
    rows = tokens // 2
    piece = rows // PARTS
    heads = width // HD
    half = HD // 2
    kvw = w_key.shape[0]
    window = rows + 128
    chips = n // 2
    zs = chips // 2
    me = lax.axis_index("weight")
    core = me % 2
    chip = me // 2
    pos = (chip // 2) * (1 - chip % 2) + (2 * zs - 1 - chip // 2) * (chip % 2)
    sib = me + 1 - 2 * core

    def chip_at(place):
        place = (place + 2 * chips) % chips
        y = place // zs
        z = place * (1 - y) + (2 * zs - 1 - place) * y
        return z * 2 + y

    def at(place):
        return chip_at(place) * 2 + core

    peers = (at(pos + 1), at(pos - 1))

    def remote(src, dst, send, recv, target):
        return pltpu.make_async_remote_copy(
            src_ref=src, dst_ref=dst, send_sem=send, recv_sem=recv,
            device_id={"weight": target}, device_id_type=pl.DeviceIdType.MESH,
        )

    def ring(way, stage, step, part):
        owner = at(pos - step) if way == 0 else at(pos + step)
        ref = buf.at[stage, owner, pl.ds(part * piece, piece)]
        return remote(
            ref, ref, ring_send.at[way, stage, step, part], ring_recv.at[way, stage, step, part],
            peers[way],
        )

    def arrival(way, stage, step, part):
        owner = at(pos - step - 1) if way == 0 else at(pos + step + 1)
        ref = buf.at[stage, owner, pl.ds(part * piece, piece)]
        return remote(
            ref, ref, ring_send.at[way, stage, step, part], ring_recv.at[way, stage, step, part],
            peers[way],
        )

    def share(stage, slot, place, own):
        owner = chip_at(place) * 2 + (core if own else 1 - core)
        ref = buf.at[stage, owner]
        return remote(ref, ref, sib_send.at[stage, slot], sib_recv.at[stage, slot], sib)

    def send_parts(stage, parts):
        for part in parts:
            for way in range(2):
                ring(way, stage, 0, part).start()

    def send_own(stage):
        send_parts(stage, range(PARTS))
        share(stage, 0, pos, True).start()

    def share_part(stage, part, own):
        owner = chip_at(pos + 4) * 2 + (core if own else 1 - core)
        ref = buf.at[stage, owner, pl.ds(part * piece, piece)]
        return remote(ref, ref, sib_send.at[stage, 7 + part], sib_recv.at[stage, 7 + part], sib)

    def kv_copy(stage, side):
        ref = kv.at[stage, side]
        return remote(ref, ref, kv_send.at[stage], kv_recv.at[stage], sib)

    own_x = [
        pltpu.make_async_copy(
            hidden.at[pl.ds(stage * rows, rows)], buf.at[stage, me], load_sem.at[4 + stage]
        )
        for stage in range(2)
    ]
    for copy in own_x:
        copy.start()
    loads = [
        pltpu.make_async_copy(src, dst, load_sem.at[i])
        for i, (src, dst) in enumerate(
            (
                (w_query, vq),
                (w_key, vkv.at[pl.ds(0, kvw)]),
                (w_value, vkv.at[pl.ds(kvw, kvw)]),
                (w_out, vo),
            )
        )
    ]
    barrier = pltpu.get_barrier_semaphore()

    def greet(i, carry):
        pl.semaphore_signal(
            barrier, inc=1, device_id={"weight": (me + 2 * i) % n},
            device_id_type=pl.DeviceIdType.MESH,
        )
        return carry

    lax.fori_loop(1, chips, greet, 0)
    pl.semaphore_signal(
        barrier, inc=1, device_id={"weight": sib}, device_id_type=pl.DeviceIdType.MESH
    )
    acc_q[...] = jnp.zeros_like(acc_q)
    acc_kv[...] = jnp.zeros_like(acc_kv)
    acc_o[...] = jnp.zeros_like(acc_o)
    kbuf[0:128] = jnp.zeros((128, HD), bf16)
    vbuf[0:128] = jnp.zeros((128, HD), bf16)
    ids = seg[...].astype(f32)
    seg_row[...] = jnp.broadcast_to(
        jnp.concatenate([jnp.full((1, 128), -1.0, f32), ids], axis=1), seg_row.shape
    )
    seg_col[...] = spread(ids, 128)
    for copy in own_x:
        copy.wait()
    for copy in loads:
        copy.start()
    pl.semaphore_wait(barrier, chips)
    send_parts(0, range(PARTS // 2))

    groups = tokens // 128
    lines = []
    for stage in range(2):
        values = buf[stage, me].astype(f32)
        sums = jnp.sum(values * values, axis=1, keepdims=True)
        across = jnp.broadcast_to(sums, (rows, 128)).T[0:1]
        lines += [across[:, i * 128:(i + 1) * 128] for i in range(rows // 128)]
    own_gain = gain[...].astype(f32).reshape(1, width)
    lines += [own_gain[:, i * 128:(i + 1) * 128] for i in range(width // 128)]
    stats[core, chip] = jnp.concatenate(lines, axis=0)

    def stat_copy(i, owner):
        ref = stats.at[core, owner]
        return remote(ref, ref, stat_send.at[i], stat_recv.at[i], (me + 2 * i) % n)

    def stat_share(side):
        ref = stats.at[side]
        return remote(ref, ref, stat_send.at[0], stat_recv.at[0], sib)

    def send_stat(i, carry):
        stat_copy(i, chip).start()
        return carry

    lax.fori_loop(1, chips, send_stat, 0)
    send_parts(0, range(PARTS // 2, PARTS))
    share(0, 0, pos, True).start()

    def prepare():
        def wait_stat(i, carry):
            stat_copy(i, (chip - i + chips) % chips).wait_recv()
            return carry

        lax.fori_loop(1, chips, wait_stat, 0)
        stat_share(core).start()
        stat_share(1 - core).wait_recv()
        total = jnp.sum(stats[0] + stats[1], axis=0)
        scale = lax.rsqrt(total / jnp.float32(n * width) + 1e-05)
        for i in range(groups):
            rcol[i * 128:(i + 1) * 128] = spread(scale[i:i + 1], 128)
        for copy in loads[:3]:
            copy.wait()

    def tables(stage):
        first = stage * rows
        lane = lax.broadcasted_iota(jnp.int32, (rows, HD), 1)
        freq = jnp.exp(
            -(2.0 * (lane % half).astype(f32) / HD) * jnp.log(jnp.float32(500000.0))
        )
        col = seg_col[pl.ds(pl.multiple_of(first, rows), rows)]
        row = seg_row[0:1, pl.ds(pl.multiple_of(first, 128), window)]
        same = jnp.concatenate([col] * (window // 128), axis=1) == row
        key_at = lax.broadcasted_iota(jnp.int32, (rows, window), 1) + (first - 128)
        query_at = lax.broadcasted_iota(jnp.int32, (rows, window), 0) + first
        bias[stage] = jnp.where(same & (key_at <= query_at), 0.0, -jnp.inf)
        start = jnp.min(
            jnp.where(same, key_at.astype(f32), jnp.float32(tokens)), axis=1, keepdims=True
        )
        token = (lax.broadcasted_iota(jnp.int32, (rows, HD), 0) + first).astype(f32)
        angle = (token - start) * freq
        cos_tab[stage] = jnp.cos(angle)
        sine = jnp.sin(angle)
        sin_tab[stage] = jnp.where(lane < half, -sine, sine)

    def turn(values, stage):
        other = jnp.concatenate([values[:, half:], values[:, :half]], axis=1)
        return (values * cos_tab[stage] + other * sin_tab[stage]).astype(bf16)

    def project(stage, owner):
        scale_rows = rcol[pl.ds(pl.multiple_of(stage * rows, rows), rows)]
        wide = jnp.concatenate([scale_rows] * (width // 128), axis=1)
        tile = stats[owner % 2, owner // 2]
        gains = jnp.concatenate(
            [tile[groups + i:groups + i + 1] for i in range(width // 128)], axis=1
        )
        block = (buf[stage, owner].astype(f32) * wide * gains).astype(bf16)
        depth = pl.ds(pl.multiple_of(owner * width, width), width)
        acc_q[stage] += dot(block, vq[depth])
        acc_kv[stage] += dot_t(block, vkv[:, depth])

    def combine(stage, owner):
        depth = pl.ds(pl.multiple_of(owner * width, width), width)
        acc_o[stage - 2] += dot(buf[stage, owner], vo[depth])

    def use(stage, owner):
        @pl.when(stage < 2)
        def _():
            project(stage, owner)

        @pl.when(stage >= 2)
        def _():
            combine(stage, owner)

    def keys_of(stage):
        kv_copy(stage, 1 - core).wait_recv()
        low, high = kv[stage, 0], kv[stage, 1]
        keys = jnp.concatenate([low[:, :half], high[:, :half]], axis=1)
        values = jnp.concatenate([low[:, half:], high[:, half:]], axis=1)
        here = pl.ds(pl.multiple_of(stage * rows + 128, 128), rows)
        kbuf[here] = turn(keys.astype(f32), stage)
        vbuf[here] = values

    def attend(stage, head):
        near = pl.ds(pl.multiple_of(stage * rows, 128), window)
        key_win = kbuf[near]
        value_win = vbuf[near]
        cols = pl.ds(pl.multiple_of(head * HD, HD), HD)
        query = turn(acc_q[stage, :, cols], stage)
        scores = dot_t(query, key_win) / jnp.sqrt(jnp.float32(HD)) + bias[stage]
        probs = jnp.exp(scores - jnp.max(scores, axis=1, keepdims=True))
        mass = jnp.sum(probs, axis=1, keepdims=True)
        buf[stage + 2, me, :, cols] = (dot(probs.astype(bf16), value_win) / mass).astype(bf16)

    def step_body(t, carry):
        stage = t // 4
        step = t % 4

        @pl.when((step == 3) & (stage < 3))
        def _():
            send_own(stage + 1)

        def one_part(part, carry):
            for way in range(2):
                @pl.when((step < 3) | (part % 2 == way))
                def _():
                    arrival(way, stage, step, part).wait_recv()

                @pl.when((step < 2) | ((step == 2) & (part % 2 == way)))
                def _():
                    ring(way, stage, step + 1, part).start()

            @pl.when(step == 3)
            def _():
                share_part(stage, part, True).start()

            @pl.when((step < 3) & (part == PARTS - 1))
            def _():
                share(stage, step + 1, pos - step - 1, True).start()
                share(stage, step + 4, pos + step + 1, True).start()

            @pl.when((t == 0) & (part == 2))
            def _():
                prepare()

            @pl.when(((t == 1) | (t == 2)) & (part == 1))
            def _():
                tables(t - 1)

            @pl.when((t == 7) & (part == 0))
            def _():
                loads[3].wait()

            head = part + 2 * step
            behind = (stage == 1) | (stage == 2)

            @pl.when(behind & (step == 0) & (part == 0))
            def _():
                keys_of(stage - 1)

            @pl.when(behind & (part < 2) & (head < heads))
            def _():
                attend(stage - 1, head)

            left = part // 2
            place = pos - step * (1 - left) + step * left
            slot = step * (1 - left) + (step + 3) * left * ((step + 2) // 3)

            @pl.when((step > 0) | (left == 1))
            def _():
                @pl.when(part % 2 == 0)
                def _():
                    share(stage, slot, place, False).wait_recv()

                use(stage, chip_at(place) * 2 + part % 2)

            return carry

        lax.fori_loop(0, PARTS, one_part, 0)

        @pl.when(step == 3)
        def _():
            for part in range(PARTS):
                share_part(stage, part, False).wait_recv()

            def far(k, carry):
                use(stage, chip_at(pos + 4) * 2 + k)
                return carry

            lax.fori_loop(0, 2, far, 0)

        @pl.when((step == 3) & (stage < 2))
        def _():
            kv[stage, core] = acc_kv[stage].astype(bf16)
            kv_copy(stage, core).start()

        return carry

    lax.fori_loop(0, 16, step_body, 0)

    for stage in range(2):
        out[stage * rows:(stage + 1) * rows] = (
            buf[stage, me].astype(f32) + acc_o[stage]
        ).astype(bf16)

    def finish(stage, carry):
        for way in range(2):
            for step in range(4):
                for part in range(PARTS):
                    if step < 3 or part % 2 == way:
                        ring(way, stage, step, part).wait_send()
        for slot, away in enumerate((0, -1, -2, -3, 1, 2, 3)):
            share(stage, slot, pos + away, True).wait_send()
        for part in range(PARTS):
            share_part(stage, part, True).wait_send()
        return carry

    lax.fori_loop(0, 4, finish, 0)
    for stage in range(2):
        kv_copy(stage, core).wait_send()

    def left(i, carry):
        stat_copy(i, chip).wait_send()
        return carry

    lax.fori_loop(1, chips, left, 0)
    stat_share(core).wait_send()


def ring_body(hidden_in, norm_gain, w_query, w_key, w_value, w_out, segment_ids):
    n = lax.axis_size("weight")
    tokens, width = hidden_in.shape
    depth = w_query.shape[0]
    rows = tokens // 2
    kvw = w_key.shape[1]
    f32, bf16 = jnp.float32, jnp.bfloat16
    anywhere = pl.BlockSpec(memory_space=pl.ANY)
    vmem = pl.BlockSpec(memory_space=pltpu.VMEM)
    dma = pltpu.SemaphoreType.DMA
    return pl.pallas_call(
        functools.partial(fused, n),
        out_shape=jax.ShapeDtypeStruct((tokens, width), bf16),
        in_specs=[anywhere, vmem, anywhere, anywhere, anywhere, anywhere, vmem],
        out_specs=vmem,
        scratch_shapes=[
            pltpu.VMEM((4, n, rows, width), bf16),
            pltpu.VMEM(w_query.shape, bf16),
            pltpu.VMEM((2 * kvw, depth), bf16),
            pltpu.VMEM(w_out.shape, bf16),
            pltpu.VMEM((2, rows, w_query.shape[1]), f32),
            pltpu.VMEM((2, rows, 2 * kvw), f32),
            pltpu.VMEM((2, rows, width), f32),
            pltpu.VMEM((2, n // 2, (tokens + width) // 128, 128), f32),
            pltpu.VMEM((tokens, 128), f32),
            pltpu.VMEM((8, tokens + 128), f32),
            pltpu.VMEM((tokens, 128), f32),
            pltpu.VMEM((2, rows, HD), f32),
            pltpu.VMEM((2, rows, HD), f32),
            pltpu.VMEM((2, rows, rows + 128), f32),
            pltpu.VMEM((2, 2, rows, 2 * kvw), bf16),
            pltpu.VMEM((tokens + 128, HD), bf16),
            pltpu.VMEM((tokens + 128, HD), bf16),
            dma((6,)),
            dma((2, 4, 4, PARTS)),
            dma((2, 4, 4, PARTS)),
            dma((4, 7 + PARTS)),
            dma((4, 7 + PARTS)),
            dma((n // 2,)),
            dma((n // 2,)),
            dma((2,)),
            dma((2,)),
        ],
        compiler_params=pltpu.CompilerParams(
            collective_id=0, has_side_effects=True, vmem_limit_bytes=56 * 1024 * 1024
        ),
    )(
        hidden_in, norm_gain, w_query, w_key.T, w_value.T, w_out, segment_ids[None, :]
    )


def solution(mesh):
    placed = (
        P("group", "weight"),
        P("weight"),
        P(None, "weight"),
        P(None, "weight"),
        P(None, "weight"),
        P(None, "weight"),
        P("group"),
    )
    chosen = ring_body if mesh.shape["weight"] == 2 * KVH else body
    return jax.shard_map(
        chosen, mesh=mesh, in_specs=placed, out_specs=P("group", "weight"), check_vma=False
    )
```

```python
import functools

import jax
import jax.numpy as jnp
from jax import lax
from jax.experimental import pallas as pl
from jax.experimental.pallas import tpu as pltpu
from jax.sharding import PartitionSpec as P

KVH = 8
PARTS = 4
HD = 128


def partner(shard, axis, bit):
    return lax.ppermute(shard, axis, [(i, i ^ 1 << bit) for i in range(lax.axis_size(axis))])


def rotate(values, position):
    half = values.shape[-1] // 2
    steps = jnp.arange(half, dtype=jnp.float32)
    freq = jnp.exp(-(2.0 * steps / (2 * half)) * jnp.log(jnp.float32(500000.0)))
    angle = position[:, None] * freq[None, :]
    cosine = jnp.cos(angle)[:, None, :]
    sine = jnp.sin(angle)[:, None, :]
    first = values[..., :half]
    second = values[..., half:]
    return jnp.concatenate(
        [first * cosine - second * sine, second * cosine + first * sine], axis=-1
    )


def add_product(piece, weights):
    return jnp.dot(piece, weights, preferred_element_type=jnp.float32)


def body(hidden_in, norm_gain, w_query, w_key, w_value, w_out, segment_ids):
    count = hidden_in.shape[0]
    as_float = hidden_in.astype(jnp.float32)
    full_rows, full_gain = (
        lax.all_gather(hidden_in, "weight", axis=1, tiled=True),
        lax.all_gather(norm_gain[None, :], "weight", axis=1, tiled=True),
    )
    rows_float = full_rows.astype(jnp.float32)
    mean_sq = jnp.mean(rows_float * rows_float, axis=1, keepdims=True)
    normed = (rows_float * lax.rsqrt(mean_sq + 1e-05) * full_gain.astype(jnp.float32)).astype(
        jnp.bfloat16
    )
    query_raw = jnp.dot(normed, w_query, preferred_element_type=jnp.float32)
    key_acc = jnp.dot(normed, w_key, preferred_element_type=jnp.float32)
    value_acc = jnp.dot(normed, w_value, preferred_element_type=jnp.float32)
    key_local = key_acc.astype(jnp.bfloat16)
    value_local = value_acc.astype(jnp.bfloat16)
    head_count = w_query.shape[1] // HD
    block_size = lax.axis_size("weight") // KVH
    my_index = lax.axis_index("weight")
    key_head, value_head = (key_local, value_local)
    for bit_number in range(block_size.bit_length() - 1):
        other_key, other_value = partner((key_head, value_head), "weight", bit_number)
        upper_half = my_index >> bit_number & 1 == 1
        key_head = jnp.where(
            upper_half,
            jnp.concatenate([other_key, key_head], axis=1),
            jnp.concatenate([key_head, other_key], axis=1),
        )
        value_head = jnp.where(
            upper_half,
            jnp.concatenate([other_value, value_head], axis=1),
            jnp.concatenate([value_head, other_value], axis=1),
        )
    index = jnp.arange(count, dtype=jnp.int32)
    same = segment_ids[:, None] == segment_ids[None, :]
    start_index = jnp.min(jnp.where(same, index[None, :], count), axis=1)
    position = (index - start_index).astype(jnp.float32)
    keep = same & (index[None, :] <= index[:, None])
    query = rotate(query_raw.reshape(count, head_count, HD), position).astype(jnp.bfloat16)
    key_rot = rotate(key_head.astype(jnp.float32).reshape(count, 1, HD), position).astype(
        jnp.bfloat16
    )[:, 0, :]
    scores = jnp.einsum(
        "thd,sd->hts", query, key_rot, preferred_element_type=jnp.float32
    ) / jnp.sqrt(jnp.float32(HD))
    scores = jnp.where(keep[None, :, :], scores, -jnp.inf)
    top = jnp.max(scores, axis=2, keepdims=True)
    probs = jnp.exp(scores - top)
    total = jnp.sum(probs, axis=2)
    weights = probs.astype(jnp.bfloat16)
    summed = jnp.einsum("hts,sd->thd", weights, value_head, preferred_element_type=jnp.float32)
    heads = (
        (summed / jnp.transpose(total)[:, :, None])
        .astype(jnp.bfloat16)
        .reshape(count, head_count * HD)
    )
    project = add_product(lax.all_gather(heads, "weight", axis=1, tiled=True), w_out)
    return (as_float + project).astype(jnp.bfloat16)


def dot(a, b):
    return jnp.dot(a, b, preferred_element_type=jnp.float32)


def dot_t(a, b):
    return lax.dot_general(
        a, b, (((1,), (1,)), ((), ())), preferred_element_type=jnp.float32
    )


def spread(row, height):
    return jnp.broadcast_to(row, (height, row.shape[1])).T


def fused(
    n, hidden, gain, w_query, w_key, w_value, w_out, seg, out,
    buf, vq, vkv, vo, acc_q, acc_kv, acc_o, stats, rcol, seg_row, seg_col, cos_tab, sin_tab, bias,
    kv, kbuf, vbuf, load_sem, ring_send, ring_recv, sib_send, sib_recv,
    stat_send, stat_recv, kv_send, kv_recv, mixed, out_sem,
):
    f32, bf16 = jnp.float32, jnp.bfloat16
    tokens, width = hidden.shape
    rows = tokens // 2
    piece = rows // PARTS
    heads = width // HD
    half = HD // 2
    kvw = w_key.shape[0]
    window = rows + 128
    chips = n // 2
    zs = chips // 2
    me = lax.axis_index("weight")
    core = me % 2
    chip = me // 2
    pos = (chip // 2) * (1 - chip % 2) + (2 * zs - 1 - chip // 2) * (chip % 2)
    sib = me + 1 - 2 * core

    def chip_at(place):
        place = (place + 2 * chips) % chips
        y = place // zs
        z = place * (1 - y) + (2 * zs - 1 - place) * y
        return z * 2 + y

    def at(place):
        return chip_at(place) * 2 + core

    peers = (at(pos + 1), at(pos - 1))

    def remote(src, dst, send, recv, target):
        return pltpu.make_async_remote_copy(
            src_ref=src, dst_ref=dst, send_sem=send, recv_sem=recv,
            device_id={"weight": target}, device_id_type=pl.DeviceIdType.MESH,
        )

    def ring(way, stage, step, part):
        owner = at(pos - step) if way == 0 else at(pos + step)
        ref = buf.at[stage, owner, pl.ds(part * piece, piece)]
        return remote(
            ref, ref, ring_send.at[way, stage, step, part], ring_recv.at[way, stage, step, part],
            peers[way],
        )

    def arrival(way, stage, step, part):
        owner = at(pos - step - 1) if way == 0 else at(pos + step + 1)
        ref = buf.at[stage, owner, pl.ds(part * piece, piece)]
        return remote(
            ref, ref, ring_send.at[way, stage, step, part], ring_recv.at[way, stage, step, part],
            peers[way],
        )

    def share(stage, slot, place, own):
        owner = chip_at(place) * 2 + (core if own else 1 - core)
        ref = buf.at[stage, owner]
        return remote(ref, ref, sib_send.at[stage, slot], sib_recv.at[stage, slot], sib)

    def send_parts(stage, parts):
        for part in parts:
            for way in range(2):
                ring(way, stage, 0, part).start()

    def send_own(stage):
        send_parts(stage, range(PARTS))
        share(stage, 0, pos, True).start()

    def share_part(stage, part, own):
        owner = chip_at(pos + 4) * 2 + (core if own else 1 - core)
        ref = buf.at[stage, owner, pl.ds(part * piece, piece)]
        return remote(ref, ref, sib_send.at[stage, 7 + part], sib_recv.at[stage, 7 + part], sib)

    def kv_copy(stage, side):
        ref = kv.at[stage, side]
        return remote(ref, ref, kv_send.at[stage], kv_recv.at[stage], sib)

    own_x = [
        pltpu.make_async_copy(
            hidden.at[pl.ds(stage * rows, rows)], buf.at[stage, me], load_sem.at[4 + stage]
        )
        for stage in range(2)
    ]
    for copy in own_x:
        copy.start()
    loads = [
        pltpu.make_async_copy(src, dst, load_sem.at[i])
        for i, (src, dst) in enumerate(
            (
                (w_query, vq),
                (w_key, vkv.at[pl.ds(0, kvw)]),
                (w_value, vkv.at[pl.ds(kvw, kvw)]),
                (w_out, vo),
            )
        )
    ]
    barrier = pltpu.get_barrier_semaphore()

    def greet(i, carry):
        pl.semaphore_signal(
            barrier, inc=1, device_id={"weight": (me + 2 * i) % n},
            device_id_type=pl.DeviceIdType.MESH,
        )
        return carry

    lax.fori_loop(1, chips, greet, 0)
    pl.semaphore_signal(
        barrier, inc=1, device_id={"weight": sib}, device_id_type=pl.DeviceIdType.MESH
    )
    acc_q[...] = jnp.zeros_like(acc_q)
    acc_kv[...] = jnp.zeros_like(acc_kv)
    acc_o[...] = jnp.zeros_like(acc_o)
    kbuf[0:128] = jnp.zeros((128, HD), bf16)
    vbuf[0:128] = jnp.zeros((128, HD), bf16)
    ids = seg[...].astype(f32)
    seg_row[...] = jnp.broadcast_to(
        jnp.concatenate([jnp.full((1, 128), -1.0, f32), ids], axis=1), seg_row.shape
    )
    seg_col[...] = spread(ids, 128)
    for copy in own_x:
        copy.wait()
    pl.semaphore_wait(barrier, chips)
    send_parts(0, range(PARTS // 2))
    for copy in loads:
        copy.start()

    groups = tokens // 128
    lines = []
    for stage in range(2):
        values = buf[stage, me].astype(f32)
        sums = jnp.sum(values * values, axis=1, keepdims=True)
        across = jnp.broadcast_to(sums, (rows, 128)).T[0:1]
        lines += [across[:, i * 128:(i + 1) * 128] for i in range(rows // 128)]
    own_gain = gain[...].astype(f32).reshape(1, width)
    lines += [own_gain[:, i * 128:(i + 1) * 128] for i in range(width // 128)]
    stats[core, chip] = jnp.concatenate(lines, axis=0)

    def stat_copy(i, owner):
        ref = stats.at[core, owner]
        return remote(ref, ref, stat_send.at[i], stat_recv.at[i], (me + 2 * i) % n)

    def stat_share(side):
        ref = stats.at[side]
        return remote(ref, ref, stat_send.at[0], stat_recv.at[0], sib)

    def send_stat(i, carry):
        stat_copy(i, chip).start()
        return carry

    lax.fori_loop(1, chips, send_stat, 0)
    send_parts(0, range(PARTS // 2, PARTS))
    share(0, 0, pos, True).start()

    def prepare():
        def wait_stat(i, carry):
            stat_copy(i, (chip - i + chips) % chips).wait_recv()
            return carry

        lax.fori_loop(1, chips, wait_stat, 0)
        stat_share(core).start()
        stat_share(1 - core).wait_recv()
        total = jnp.sum(stats[0] + stats[1], axis=0)
        scale = lax.rsqrt(total / jnp.float32(n * width) + 1e-05)
        for i in range(groups):
            rcol[i * 128:(i + 1) * 128] = spread(scale[i:i + 1], 128)
        for copy in loads[:3]:
            copy.wait()

    def tables(stage):
        first = stage * rows
        lane = lax.broadcasted_iota(jnp.int32, (rows, HD), 1)
        freq = jnp.exp(
            -(2.0 * (lane % half).astype(f32) / HD) * jnp.log(jnp.float32(500000.0))
        )
        col = seg_col[pl.ds(pl.multiple_of(first, rows), rows)]
        row = seg_row[0:1, pl.ds(pl.multiple_of(first, 128), window)]
        same = jnp.concatenate([col] * (window // 128), axis=1) == row
        key_at = lax.broadcasted_iota(jnp.int32, (rows, window), 1) + (first - 128)
        query_at = lax.broadcasted_iota(jnp.int32, (rows, window), 0) + first
        bias[stage] = jnp.where(same & (key_at <= query_at), 0.0, -jnp.inf)
        start = jnp.min(
            jnp.where(same, key_at.astype(f32), jnp.float32(tokens)), axis=1, keepdims=True
        )
        token = (lax.broadcasted_iota(jnp.int32, (rows, HD), 0) + first).astype(f32)
        angle = (token - start) * freq
        cos_tab[stage] = jnp.cos(angle)
        sine = jnp.sin(angle)
        sin_tab[stage] = jnp.where(lane < half, -sine, sine)

    def turn(values, stage):
        other = jnp.concatenate([values[:, half:], values[:, :half]], axis=1)
        return (values * cos_tab[stage] + other * sin_tab[stage]).astype(bf16)

    def project(stage, owner):
        scale_rows = rcol[pl.ds(pl.multiple_of(stage * rows, rows), rows)]
        wide = jnp.concatenate([scale_rows] * (width // 128), axis=1)
        tile = stats[owner % 2, owner // 2]
        gains = jnp.concatenate(
            [tile[groups + i:groups + i + 1] for i in range(width // 128)], axis=1
        )
        block = (buf[stage, owner].astype(f32) * wide * gains).astype(bf16)
        depth = pl.ds(pl.multiple_of(owner * width, width), width)
        acc_q[stage] += dot(block, vq[depth])
        acc_kv[stage] += dot_t(block, vkv[:, depth])

    def combine(stage, owner):
        depth = pl.ds(pl.multiple_of(owner * width, width), width)
        acc_o[stage - 2] += dot(buf[stage, owner], vo[depth])

    def use(stage, owner):
        @pl.when(stage < 2)
        def _():
            project(stage, owner)

        @pl.when(stage >= 2)
        def _():
            combine(stage, owner)

    def keys_of(stage):
        kv_copy(stage, 1 - core).wait_recv()
        low, high = kv[stage, 0], kv[stage, 1]
        keys = jnp.concatenate([low[:, :half], high[:, :half]], axis=1)
        values = jnp.concatenate([low[:, half:], high[:, half:]], axis=1)
        here = pl.ds(pl.multiple_of(stage * rows + 128, 128), rows)
        kbuf[here] = turn(keys.astype(f32), stage)
        vbuf[here] = values

    def attend(stage, head):
        near = pl.ds(pl.multiple_of(stage * rows, 128), window)
        key_win = kbuf[near]
        value_win = vbuf[near]
        cols = pl.ds(pl.multiple_of(head * HD, HD), HD)
        query = turn(acc_q[stage, :, cols], stage)
        scores = dot_t(query, key_win) / jnp.sqrt(jnp.float32(HD)) + bias[stage]
        probs = jnp.exp(scores - jnp.max(scores, axis=1, keepdims=True))
        mass = jnp.sum(probs, axis=1, keepdims=True)
        buf[stage + 2, me, :, cols] = (dot(probs.astype(bf16), value_win) / mass).astype(bf16)

    def result(stage):
        here = pl.ds(stage * rows, rows)
        return pltpu.make_async_copy(mixed.at[here], out.at[here], out_sem.at[stage])

    def step_body(t, carry):
        stage = t // 4
        step = t % 4

        @pl.when((step == 3) & (stage < 3))
        def _():
            send_own(stage + 1)

        def one_part(part, carry):
            for way in range(2):
                @pl.when((step < 3) | (part % 2 == way))
                def _():
                    arrival(way, stage, step, part).wait_recv()

                @pl.when((step < 2) | ((step == 2) & (part % 2 == way)))
                def _():
                    ring(way, stage, step + 1, part).start()

            @pl.when(step == 3)
            def _():
                share_part(stage, part, True).start()

            @pl.when((step < 3) & (part == PARTS - 1))
            def _():
                share(stage, step + 1, pos - step - 1, True).start()
                share(stage, step + 4, pos + step + 1, True).start()

            @pl.when((t == 0) & (part == 2))
            def _():
                prepare()

            @pl.when(((t == 1) | (t == 2)) & (part == 1))
            def _():
                tables(t - 1)

            @pl.when((t == 7) & (part == 0))
            def _():
                loads[3].wait()

            head = part + 2 * step
            behind = (stage == 1) | (stage == 2)

            @pl.when(behind & (step == 0) & (part == 0))
            def _():
                keys_of(stage - 1)

            @pl.when(behind & (part < 2) & (head < heads))
            def _():
                attend(stage - 1, head)

            left = part // 2
            place = pos - step * (1 - left) + step * left
            slot = step * (1 - left) + (step + 3) * left * ((step + 2) // 3)

            @pl.when((step > 0) | (left == 1))
            def _():
                @pl.when(part % 2 == 0)
                def _():
                    share(stage, slot, place, False).wait_recv()

                use(stage, chip_at(place) * 2 + part % 2)

            return carry

        lax.fori_loop(0, PARTS, one_part, 0)

        @pl.when(step == 3)
        def _():
            for part in range(PARTS):
                share_part(stage, part, False).wait_recv()

            def far(k, carry):
                use(stage, chip_at(pos + 4) * 2 + k)
                return carry

            lax.fori_loop(0, 2, far, 0)

            @pl.when(stage >= 2)
            def _():
                own = stage - 2
                mixed[pl.ds(pl.multiple_of(own * rows, rows), rows)] = (
                    buf[own, me].astype(f32) + acc_o[own]
                ).astype(bf16)

            @pl.when(stage == 2)
            def _():
                result(0).start()

        @pl.when((step == 3) & (stage < 2))
        def _():
            kv[stage, core] = acc_kv[stage].astype(bf16)
            kv_copy(stage, core).start()

        return carry

    lax.fori_loop(0, 16, step_body, 0)

    result(1).start()
    result(0).wait()
    result(1).wait()

    def finish(stage, carry):
        for way in range(2):
            for step in range(4):
                for part in range(PARTS):
                    if step < 3 or part % 2 == way:
                        ring(way, stage, step, part).wait_send()
        for slot, away in enumerate((0, -1, -2, -3, 1, 2, 3)):
            share(stage, slot, pos + away, True).wait_send()
        for part in range(PARTS):
            share_part(stage, part, True).wait_send()
        return carry

    lax.fori_loop(0, 4, finish, 0)
    for stage in range(2):
        kv_copy(stage, core).wait_send()

    def left(i, carry):
        stat_copy(i, chip).wait_send()
        return carry

    lax.fori_loop(1, chips, left, 0)
    stat_share(core).wait_send()


def ring_body(hidden_in, norm_gain, w_query, w_key, w_value, w_out, segment_ids):
    n = lax.axis_size("weight")
    tokens, width = hidden_in.shape
    depth = w_query.shape[0]
    rows = tokens // 2
    kvw = w_key.shape[1]
    f32, bf16 = jnp.float32, jnp.bfloat16
    anywhere = pl.BlockSpec(memory_space=pl.ANY)
    vmem = pl.BlockSpec(memory_space=pltpu.VMEM)
    dma = pltpu.SemaphoreType.DMA
    return pl.pallas_call(
        functools.partial(fused, n),
        out_shape=jax.ShapeDtypeStruct((tokens, width), bf16),
        in_specs=[anywhere, vmem, anywhere, anywhere, anywhere, anywhere, vmem],
        out_specs=anywhere,
        scratch_shapes=[
            pltpu.VMEM((4, n, rows, width), bf16),
            pltpu.VMEM(w_query.shape, bf16),
            pltpu.VMEM((2 * kvw, depth), bf16),
            pltpu.VMEM(w_out.shape, bf16),
            pltpu.VMEM((2, rows, w_query.shape[1]), f32),
            pltpu.VMEM((2, rows, 2 * kvw), f32),
            pltpu.VMEM((2, rows, width), f32),
            pltpu.VMEM((2, n // 2, (tokens + width) // 128, 128), f32),
            pltpu.VMEM((tokens, 128), f32),
            pltpu.VMEM((8, tokens + 128), f32),
            pltpu.VMEM((tokens, 128), f32),
            pltpu.VMEM((2, rows, HD), f32),
            pltpu.VMEM((2, rows, HD), f32),
            pltpu.VMEM((2, rows, rows + 128), f32),
            pltpu.VMEM((2, 2, rows, 2 * kvw), bf16),
            pltpu.VMEM((tokens + 128, HD), bf16),
            pltpu.VMEM((tokens + 128, HD), bf16),
            dma((6,)),
            dma((2, 4, 4, PARTS)),
            dma((2, 4, 4, PARTS)),
            dma((4, 7 + PARTS)),
            dma((4, 7 + PARTS)),
            dma((n // 2,)),
            dma((n // 2,)),
            dma((2,)),
            dma((2,)),
            pltpu.VMEM((tokens, width), bf16),
            dma((2,)),
        ],
        compiler_params=pltpu.CompilerParams(
            collective_id=0, has_side_effects=True, vmem_limit_bytes=56 * 1024 * 1024
        ),
    )(
        hidden_in, norm_gain, w_query, w_key.T, w_value.T, w_out, segment_ids[None, :]
    )


def solution(mesh):
    placed = (
        P("group", "weight"),
        P("weight"),
        P(None, "weight"),
        P(None, "weight"),
        P(None, "weight"),
        P(None, "weight"),
        P("group"),
    )
    chosen = ring_body if mesh.shape["weight"] == 2 * KVH else body
    return jax.shard_map(
        chosen, mesh=mesh, in_specs=placed, out_specs=P("group", "weight"), check_vma=False
    )
```
